32 devices in a mesh: ex: 8 (over y, x, core), feat: 4 (over z).
Axes of the slice: x: 2, y: 2, z: 4, core: 2. Of those that a mesh axis runs over, the one named last changes fastest.
Arguments:
- train_grads: bfloat16 [8192, 16384], P('ex', 'feat'), may hold values from -200 to 200
- target_grads: bfloat16 [128, 16384], P('ex', 'feat'), may hold values from -300 to 300
- target_mass: float32 [128], replicated, may hold values from 0.25 to 4
Outputs:
- mixtures: bfloat16 [128, 16384], P('ex', 'feat')
The draws below stay inside these ranges and needn't reach their ends.
All inputs are finite; a program needn't handle non-finite values.
Results may differ from the reference program's by a relative error of at most 0.0048.
Values may be sent and summed in bfloat16 or wider, within the bound.
A program may use at most 64 MiB of HBM per device.

```python
import math
import jax
import jax.numpy as jnp
from jax import lax

F = 16384
ITERS = 3
NTR = 8192
NT = 128


def draw_pair(key):
    base = jax.random.fold_in(key, 11)
    keys = jax.random.split(base, 2)
    train = jnp.clip(jax.random.normal(keys[0], (NTR, F), jnp.float32), -6.0, 6.0)
    target = jnp.clip(jax.random.normal(keys[1], (NT, F), jnp.float32), -6.0, 6.0)
    return (train, target)


def draw_train_grads(key, part):
    return draw_pair(key)[0].astype(jnp.bfloat16)


def draw_target_grads(key, part):
    return draw_pair(key)[1].astype(jnp.bfloat16)


def setup_inputs(seed: int = 0) -> dict:
    arg_keys = jax.random.split(jax.random.key(seed), 4)
    train_grads = draw_train_grads(jax.random.fold_in(arg_keys[3], 71), 0)
    target_grads = draw_target_grads(jax.random.fold_in(arg_keys[3], 71), 0)
    target_mass = jnp.clip(jnp.exp(jax.random.uniform(arg_keys[2], (NT,), jnp.float32, math.log(0.25), math.log(4.0))), 0.25, 4.0)
    return dict(train_grads=train_grads, target_grads=target_grads, target_mass=target_mass)


def log_sum_exp(values, axis):
    top = lax.optimization_barrier(jnp.max(values, axis=axis, keepdims=True))
    total = lax.optimization_barrier(jnp.sum(jnp.exp(values - top), axis=axis))
    return jnp.squeeze(top, axis) + jnp.log(total)

def reference(train_grads, target_grads, target_mass):
    scale = 3.0 / math.sqrt(F)
    logits = jnp.dot(train_grads, target_grads.T, preferred_element_type=jnp.float32) * scale
    mass_total = jnp.sum(target_mass)
    weights = target_mass / mass_total
    log_b = jnp.log(target_mass) - jnp.log(mass_total)
    log_a = -math.log(NTR)
    col_pot = jnp.zeros((NT,), jnp.float32)
    row_pot = jnp.zeros((NTR,), jnp.float32)
    for step in range(ITERS):
        row_pot = log_a - log_sum_exp(logits + col_pot[None, :], 1)
        col_pot = log_b - log_sum_exp(logits + row_pot[:, None], 0)
    plan = jnp.exp(logits + row_pot[:, None] + col_pot[None, :]).astype(jnp.bfloat16)
    mixed = jnp.dot(plan.T, train_grads, preferred_element_type=jnp.float32)
    return (mixed / weights[:, None]).astype(jnp.bfloat16)
```

```python
import functools
import math

import jax
import jax.numpy as jnp
from jax import lax
from jax.experimental import pallas as pl
from jax.experimental.pallas import tpu as pltpu
from jax.sharding import PartitionSpec as P

ITERS = 3
MESH = pl.DeviceIdType.MESH


def remote(src, dst, send, recv, axis, peer):
    return pltpu.make_async_remote_copy(
        src_ref=src,
        dst_ref=dst,
        send_sem=send,
        recv_sem=recv,
        device_id={axis: peer},
        device_id_type=MESH,
    )


def kernel(
    n, nf, chunks,
    train_hbm, target, mass_row, mass_col, out,
    train, tg, part, rs, logits, plan_t, macc, mb, mr, st_send, st_recv,
    load_sem, g_send, g_recv, r_send, r_recv, a_send, a_recv, s_send, s_recv, m_send, m_recv,
):
    me = lax.axis_index("ex")
    mf = lax.axis_index("feat")
    rows, depth = train.shape
    nt = tg.shape[0]
    t = target.shape[0]
    dc = depth // chunks
    rf = rows // nf
    scale = 3.0 / math.sqrt(depth * nf)
    log_a = -math.log(rows * n)

    def ex_at(k):
        return lax.rem(me + k, n)

    def feat_at(k):
        return lax.rem(mf + k, nf)

    def block(index, size):
        return pl.ds(pl.multiple_of(index * size, size), size)

    loads = []
    for c in range(chunks):
        cols = pl.ds(c * dc, dc)
        loads.append(
            pltpu.make_async_copy(train_hbm.at[:, cols], train.at[:, cols], load_sem.at[c])
        )
        loads[-1].start()

    barrier = pltpu.get_barrier_semaphore()
    for k in range(1, n):
        pl.semaphore_signal(barrier, inc=1, device_id={"ex": ex_at(k)}, device_id_type=MESH)
    for k in range(1, nf):
        pl.semaphore_signal(barrier, inc=1, device_id={"feat": feat_at(k)}, device_id_type=MESH)
    pl.semaphore_wait(barrier, n + nf - 2)

    gathers = []
    for c in range(chunks):
        cols = pl.ds(c * dc, dc)
        for k in range(1, n):
            copy = remote(
                target.at[:, cols], tg.at[block(me, t), cols],
                g_send.at[c, k], g_recv.at[c, k], "ex", ex_at(k),
            )
            copy.start()
            gathers.append(copy)
    tg[block(me, t), :] = target[...]

    mass_total = jnp.sum(mass_row[...], axis=1, keepdims=True)
    log_b = jnp.log(mass_row[...]) - jnp.log(mass_total)

    def score(c, index):
        where = block(index, rf)
        value = lax.dot_general(
            train[where, c * dc:(c + 1) * dc],
            tg[:, c * dc:(c + 1) * dc],
            (((1,), (1,)), ((), ())),
            preferred_element_type=jnp.float32,
        )
        if c == 0:
            part[where, :] = value
        else:
            part[where, :] += value

    reduces = []
    for c in range(chunks):
        loads[c].wait()
        for k in range(1, n):
            gathers[c * (n - 1) + k - 1].wait_recv()
        if c < chunks - 1:
            @pl.loop(0, nf)
            def _(index):
                score(c, index)
        else:
            for k in range(1, nf):
                score(c, feat_at(k))
                copy = remote(
                    part.at[block(feat_at(k), rf)], rs.at[k], r_send.at[k], r_recv.at[k], "feat", feat_at(k)
                )
                copy.start()
                reduces.append(copy)
            score(c, mf)
    for copy in reduces:
        copy.wait_recv()
    own = part[block(mf, rf), :]
    for k in range(1, nf):
        own = own + rs[k]
    logits[block(mf, rf), :] = own * scale
    spreads = []
    for k in range(1, nf):
        copy = remote(
            logits.at[block(mf, rf)], logits.at[block(mf, rf)], a_send.at[k], a_recv.at[k], "feat", feat_at(k)
        )
        copy.start()
        spreads.append(copy)
    for copy in spreads:
        copy.wait_recv()

    col_pot = jnp.zeros((1, nt), jnp.float32)
    stats = []
    row_pot = None
    for step in range(ITERS):
        value = logits[...] + col_pot
        top = jnp.max(value, axis=1, keepdims=True)
        row_pot = log_a - (top + jnp.log(jnp.sum(jnp.exp(value - top), axis=1, keepdims=True)))
        value = logits[...] + row_pot
        top = jnp.max(value, axis=0, keepdims=True)
        total = jnp.sum(jnp.exp(value - top), axis=0, keepdims=True)
        st_send[step, 0:1, :] = top
        st_send[step, 1:2, :] = total
        wave = []
        for k in range(1, n):
            copy = remote(
                st_send.at[step], st_recv.at[step, me],
                s_send.at[step, k], s_recv.at[step, k], "ex", ex_at(k),
            )
            copy.start()
            wave.append(copy)
        st_recv[step, me] = st_send[step]
        for copy in wave:
            copy.wait_recv()
        stats += wave
        tops = st_recv[step, :, 0, :]
        totals = st_recv[step, :, 1, :]
        top = jnp.max(tops, axis=0, keepdims=True)
        total = jnp.sum(totals * jnp.exp(tops - top), axis=0, keepdims=True)
        col_pot = log_b - (top + jnp.log(total))

    plan = jnp.exp(logits[...] + row_pot + col_pot)
    plan_t[...] = plan.T.astype(jnp.bfloat16)

    tile = math.gcd(dc, 256)
    mixes = []
    for c in range(chunks):
        cols = pl.ds(c * dc, dc)

        @pl.loop(0, dc // tile)
        def _(index):
            where = pl.ds(pl.multiple_of(c * dc + index * tile, tile), tile)
            value = jnp.dot(plan_t[...], train[:, where], preferred_element_type=jnp.float32)
            macc[:, where] = value
            mb[:, where] = value.astype(jnp.bfloat16)

        for k in range(1, n):
            copy = remote(
                mb.at[block(ex_at(k), t), cols], mr.at[me, :, cols],
                m_send.at[c, k], m_recv.at[c, k], "ex", ex_at(k),
            )
            copy.start()
            mixes.append(copy)

    weight = mass_col[block(me, t), :] / mass_total
    for c in range(chunks):
        for k in range(1, n):
            mixes[c * (n - 1) + k - 1].wait_recv()
        total = macc[block(me, t), c * dc:(c + 1) * dc]
        for k in range(1, n):
            total = total + mr[ex_at(k), :, c * dc:(c + 1) * dc].astype(jnp.float32)
        out[:, c * dc:(c + 1) * dc] = (total / weight).astype(jnp.bfloat16)
    for copy in gathers + reduces + spreads + stats + mixes:
        copy.wait_send()


def shards(train_grads, target_grads, target_mass):
    n, nf = lax.axis_size("ex"), lax.axis_size("feat")
    rows, depth = train_grads.shape
    t = target_grads.shape[0]
    nt = t * n
    chunks = 4 if depth % 512 == 0 else 1
    f32, bf16 = jnp.float32, jnp.bfloat16
    vmem = pl.BlockSpec(memory_space=pltpu.VMEM)
    dma = pltpu.SemaphoreType.DMA
    return pl.pallas_call(
        functools.partial(kernel, n, nf, chunks),
        out_shape=jax.ShapeDtypeStruct((t, depth), bf16),
        in_specs=[pl.BlockSpec(memory_space=pl.ANY), vmem, vmem, vmem],
        out_specs=vmem,
        scratch_shapes=[
            pltpu.VMEM((rows, depth), bf16),
            pltpu.VMEM((nt, depth), bf16),
            pltpu.VMEM((rows, nt), f32),
            pltpu.VMEM((nf, rows // nf, nt), f32),
            pltpu.VMEM((rows, nt), f32),
            pltpu.VMEM((nt, rows), bf16),
            pltpu.VMEM((nt, depth), f32),
            pltpu.VMEM((nt, depth), bf16),
            pltpu.VMEM((n, t, depth), bf16),
            pltpu.VMEM((ITERS, 8, nt), f32),
            pltpu.VMEM((ITERS, n, 8, nt), f32),
            dma((chunks,)),
            dma((chunks, n)), dma((chunks, n)),
            dma((nf,)), dma((nf,)),
            dma((nf,)), dma((nf,)),
            dma((ITERS, n)), dma((ITERS, n)),
            dma((chunks, n)), dma((chunks, n)),
        ],
        compiler_params=pltpu.CompilerParams(
            collective_id=0, has_side_effects=True, vmem_limit_bytes=48 * 1024 * 1024
        ),
        cost_estimate=pl.CostEstimate(
            flops=4 * rows * nt * depth,
            bytes_accessed=2 * rows * depth,
            transcendentals=7 * rows * nt,
        ),
    )(train_grads, target_grads, target_mass.reshape(1, nt), target_mass.reshape(nt, 1))


def solution(mesh):
    return jax.shard_map(
        shards,
        mesh=mesh,
        in_specs=(P("ex", "feat"), P("ex", "feat"), P()),
        out_specs=P("ex", "feat"),
        check_vma=False,
    )
```

```python
import functools
import math

import jax
import jax.numpy as jnp
from jax import lax
from jax.experimental import pallas as pl
from jax.experimental.pallas import tpu as pltpu
from jax.sharding import PartitionSpec as P

ITERS = 3
MESH = pl.DeviceIdType.MESH


def remote(src, dst, send, recv, axis, peer):
    return pltpu.make_async_remote_copy(
        src_ref=src,
        dst_ref=dst,
        send_sem=send,
        recv_sem=recv,
        device_id={axis: peer},
        device_id_type=MESH,
    )


def kernel(
    n, nf, chunks,
    train_hbm, target, mass_hbm, out,
    train, tg, part, rs, plan_t, macc, mb, xr, cb, mr, mass_row, mass_col,
    ft_send, ft_recv, ex_send, ex_recv,
    load_sem, own_sem, mass_sem, g_send, g_recv, f_send, f_recv, r_send, r_recv,
    t_send, t_recv, s_send, s_recv, a_send, a_recv, x_send, x_recv, m_send, m_recv,
):
    me = lax.axis_index("ex")
    mf = lax.axis_index("feat")
    rows, depth = train.shape
    nt = tg.shape[0]
    t = target.shape[0]
    dc = depth // chunks
    rf = rows // nf
    nq = n // 2
    q = me // 2
    core = lax.rem(me, 2)
    sibling = me + 1 - 2 * core
    scale = 3.0 / math.sqrt(depth * nf)
    log_a = -math.log(rows * n)

    def ex_at(k):
        return lax.rem(me + k, n)

    def feat_at(k):
        return lax.rem(mf + k, nf)

    def chip_at(j):
        return lax.rem(q + j, nq)

    def chip_from(j):
        return lax.rem(q - j + nq, nq)

    def block(index, size):
        return pl.ds(pl.multiple_of(index * size, size), size)

    def span(c):
        return pl.ds(c * dc, dc)

    mass_load = pltpu.make_async_copy(mass_hbm, mass_row, mass_sem)
    mass_load.start()
    own_load = pltpu.make_async_copy(target, tg.at[block(me, t)], own_sem)
    own_load.start()
    loads = []
    for c in range(chunks):
        loads.append(
            pltpu.make_async_copy(train_hbm.at[:, span(c)], train.at[:, span(c)], load_sem.at[c])
        )
        loads[-1].start()

    barrier = pltpu.get_barrier_semaphore()
    for k in range(1, n):
        pl.semaphore_signal(barrier, inc=1, device_id={"ex": ex_at(k)}, device_id_type=MESH)
    for k in range(1, nf):
        pl.semaphore_signal(barrier, inc=1, device_id={"feat": feat_at(k)}, device_id_type=MESH)
    pl.semaphore_wait(barrier, n + nf - 2)

    gathers = []
    forwards = []
    for c in range(chunks):
        for j in range(1, nq):
            copy = remote(
                target.at[:, span(c)], tg.at[block(me, t), span(c)],
                g_send.at[c, j], g_recv.at[c, j], "ex", 2 * chip_at(j) + core,
            )
            copy.start()
            gathers.append(copy)
        copy = remote(
            target.at[:, span(c)], tg.at[block(me, t), span(c)],
            f_send.at[c, 0], f_recv.at[c, 0], "ex", sibling,
        )
        copy.start()
        forwards.append([copy])

    mass_load.wait()
    mass_total = jnp.sum(mass_row[...], axis=1, keepdims=True)
    log_b = jnp.log(mass_row[...]) - jnp.log(mass_total)
    mass_col[...] = jnp.broadcast_to(mass_row[...] / mass_total, (8, nt)).T
    own_load.wait()

    def forward(c):
        for j in range(1, nq):
            gathers[c * (nq - 1) + j - 1].wait_recv()
            where = block(2 * chip_from(j) + core, t)
            copy = remote(
                tg.at[where, span(c)], tg.at[where, span(c)],
                f_send.at[c, j], f_recv.at[c, j], "ex", sibling,
            )
            copy.start()
            forwards[c].append(copy)

    def score(c, index):
        where = block(index, rf)
        value = lax.dot_general(
            train[where, c * dc:(c + 1) * dc],
            tg[:, c * dc:(c + 1) * dc],
            (((1,), (1,)), ((), ())),
            preferred_element_type=jnp.float32,
        )
        if c == 0:
            part[where, :] = value
        else:
            part[where, :] += value

    reduces = []
    forward(0)
    for c in range(chunks):
        if c + 1 < chunks:
            forward(c + 1)
        loads[c].wait()
        for copy in forwards[c]:
            copy.wait_recv()
        if c < chunks - 1:
            @pl.loop(0, nf)
            def _(index):
                score(c, index)
        else:
            for k in range(1, nf):
                score(c, feat_at(k))
                copy = remote(
                    part.at[block(feat_at(k), rf)], rs.at[k],
                    r_send.at[k], r_recv.at[k], "feat", feat_at(k),
                )
                copy.start()
                reduces.append(copy)
            score(c, mf)
    logits = part[block(mf, rf), :]
    for copy in reduces:
        copy.wait_recv()
    for k in range(1, nf):
        logits = logits + rs[k]
    logits = logits * scale
    part[block(mf, rf), :] = logits

    def exchange(step, axis, send, recv, here, at, size, send_sem, recv_sem, top, total):
        send[step, 0:1, :] = top
        send[step, 1:2, :] = total
        wave = []
        for k in range(1, size):
            copy = remote(
                send.at[step], recv.at[step, here],
                send_sem.at[step, k], recv_sem.at[step, k], axis, at(k),
            )
            copy.start()
            wave.append(copy)
        recv[step, here] = send[step]
        for copy in wave:
            copy.wait_recv()
        tops = recv[step, :, 0, :]
        top = jnp.max(tops, axis=0, keepdims=True)
        total = jnp.sum(recv[step, :, 1, :] * jnp.exp(tops - top), axis=0, keepdims=True)
        return top, total, wave

    col_pot = jnp.zeros((1, nt), jnp.float32)
    stats = []
    row_pot = None
    for step in range(ITERS):
        value = logits + col_pot
        top = jnp.max(value, axis=1, keepdims=True)
        row_pot = log_a - (top + jnp.log(jnp.sum(jnp.exp(value - top), axis=1, keepdims=True)))
        value = logits + row_pot
        top = jnp.max(value, axis=0, keepdims=True)
        total = jnp.sum(jnp.exp(value - top), axis=0, keepdims=True)
        top, total, wave = exchange(
            step, "feat", ft_send, ft_recv, mf, feat_at, nf, t_send, t_recv, top, total
        )
        stats += wave
        top, total, wave = exchange(
            step, "ex", ex_send, ex_recv, me, ex_at, n, s_send, s_recv, top, total
        )
        stats += wave
        col_pot = log_b - (top + jnp.log(total))

    plan_t[mf] = jnp.exp(logits + row_pot + col_pot).T.astype(jnp.bfloat16)
    spreads = []
    for k in range(1, nf):
        copy = remote(
            plan_t.at[mf], plan_t.at[mf], a_send.at[k], a_recv.at[k], "feat", feat_at(k)
        )
        copy.start()
        spreads.append(copy)
    for copy in spreads:
        copy.wait_recv()

    tile = math.gcd(dc, 256)
    swaps = []
    mixes = []

    def mix(c):
        @pl.loop(0, dc // tile)
        def _(index):
            where = pl.ds(pl.multiple_of(c * dc + index * tile, tile), tile)
            value = jnp.zeros((nt, tile), jnp.float32)
            for f in range(nf):
                value += jnp.dot(
                    plan_t[f], train[f * rf:(f + 1) * rf, where],
                    preferred_element_type=jnp.float32,
                )
            value = value.reshape(nq, 2, t, tile)
            macc[:, :, :, where] = value
            mb[:, :, :, where] = value.astype(jnp.bfloat16)

        copy = remote(
            mb.at[:, 1 - core, :, span(c)], xr.at[:, :, span(c)],
            x_send.at[c], x_recv.at[c], "ex", sibling,
        )
        copy.start()
        swaps.append(copy)

    def send_on(c):
        cols = slice(c * dc, (c + 1) * dc)
        swaps[c].wait_recv()
        total = macc[:, core, :, cols] + xr[:, :, cols].astype(jnp.float32)
        cb[:, :, cols] = total.astype(jnp.bfloat16)
        for j in range(1, nq):
            copy = remote(
                cb.at[chip_at(j), :, span(c)], mr.at[q, :, span(c)],
                m_send.at[c, j], m_recv.at[c, j], "ex", 2 * chip_at(j) + core,
            )
            copy.start()
            mixes.append(copy)

    for c in range(chunks):
        mix(c)
        if c > 0:
            send_on(c - 1)
    send_on(chunks - 1)

    weight = mass_col[block(me, t), 0:1]
    for c in range(chunks):
        cols = slice(c * dc, (c + 1) * dc)
        total = macc[q, core, :, cols] + xr[q, :, cols].astype(jnp.float32)
        for j in range(1, nq):
            mixes[c * (nq - 1) + j - 1].wait_recv()
        for j in range(1, nq):
            total = total + mr[chip_at(j), :, cols].astype(jnp.float32)
        out[:, cols] = (total / weight).astype(jnp.bfloat16)
    for group in forwards:
        for copy in group:
            copy.wait_send()
    for copy in gathers + reduces + spreads + stats + swaps + mixes:
        copy.wait_send()


def shards(train_grads, target_grads, target_mass):
    n, nf = lax.axis_size("ex"), lax.axis_size("feat")
    rows, depth = train_grads.shape
    t = target_grads.shape[0]
    nt = t * n
    nq = n // 2
    chunks = 4 if depth % 512 == 0 else 1
    f32, bf16 = jnp.float32, jnp.bfloat16
    vmem = pl.BlockSpec(memory_space=pltpu.VMEM)
    anywhere = pl.BlockSpec(memory_space=pl.ANY)
    dma = pltpu.SemaphoreType.DMA
    return pl.pallas_call(
        functools.partial(kernel, n, nf, chunks),
        out_shape=jax.ShapeDtypeStruct((t, depth), bf16),
        in_specs=[anywhere, anywhere, anywhere],
        out_specs=vmem,
        scratch_shapes=[
            pltpu.VMEM((rows, depth), bf16),
            pltpu.VMEM((nt, depth), bf16),
            pltpu.VMEM((rows, nt), f32),
            pltpu.VMEM((nf, rows // nf, nt), f32),
            pltpu.VMEM((nf, nt, rows // nf), bf16),
            pltpu.VMEM((nq, 2, t, depth), f32),
            pltpu.VMEM((nq, 2, t, depth), bf16),
            pltpu.VMEM((nq, t, depth), bf16),
            pltpu.VMEM((nq, t, depth), bf16),
            pltpu.VMEM((nq, t, depth), bf16),
            pltpu.VMEM((1, nt), f32),
            pltpu.VMEM((nt, 8), f32),
            pltpu.VMEM((ITERS, 8, nt), f32),
            pltpu.VMEM((ITERS, nf, 8, nt), f32),
            pltpu.VMEM((ITERS, 8, nt), f32),
            pltpu.VMEM((ITERS, n, 8, nt), f32),
            dma((chunks,)), dma, dma,
            dma((chunks, nq)), dma((chunks, nq)),
            dma((chunks, nq)), dma((chunks, nq)),
            dma((nf,)), dma((nf,)),
            dma((ITERS, nf)), dma((ITERS, nf)),
            dma((ITERS, n)), dma((ITERS, n)),
            dma((nf,)), dma((nf,)),
            dma((chunks,)), dma((chunks,)),
            dma((chunks, nq)), dma((chunks, nq)),
        ],
        compiler_params=pltpu.CompilerParams(
            collective_id=0, has_side_effects=True, vmem_limit_bytes=48 * 1024 * 1024
        ),
        cost_estimate=pl.CostEstimate(
            flops=4 * rows * nt * depth,
            bytes_accessed=2 * rows * depth,
            transcendentals=7 * rows * nt,
        ),
    )(train_grads, target_grads, target_mass.reshape(1, nt))


def solution(mesh):
    return jax.shard_map(
        shards,
        mesh=mesh,
        in_specs=(P("ex", "feat"), P("ex", "feat"), P()),
        out_specs=P("ex", "feat"),
        check_vma=False,
    )
```

```python
import functools
import math

import jax
import jax.numpy as jnp
from jax import lax
from jax.experimental import pallas as pl
from jax.experimental.pallas import tpu as pltpu
from jax.sharding import PartitionSpec as P

ITERS = 3
DIRECT = 64
MESH = pl.DeviceIdType.MESH


def remote(src, dst, send, recv, axis, peer):
    return pltpu.make_async_remote_copy(
        src_ref=src,
        dst_ref=dst,
        send_sem=send,
        recv_sem=recv,
        device_id=peer if axis is None else {axis: peer},
        device_id_type=MESH,
    )


def kernel(
    n, nf, chunks,
    train_hbm, target, mass_hbm, out,
    train, tg, part, rs, scores, expo, plan_t, macc, mb, xr, cb, mr, mass_row, mass_col,
    ft_send, ft_recv, ex_send, ex_recv,
    load_sem, own_sem, mass_sem, g_send, g_recv, f_send, f_recv, r_send, r_recv,
    t_send, t_recv, s_send, s_recv, a_send, a_recv, x_send, x_recv, m_send, m_recv,
):
    me = lax.axis_index("ex")
    mf = lax.axis_index("feat")
    rows, depth = train.shape
    nt = tg.shape[0]
    t = target.shape[0]
    dc = depth // chunks
    rf = rows // nf
    nq = n // 2
    q = me // 2
    core = lax.rem(me, 2)
    sibling = me + 1 - 2 * core
    scale = 3.0 / math.sqrt(depth * nf)
    log_a = -math.log(rows * n)

    def ex_at(k):
        return lax.rem(me + k, n)

    def feat_at(k):
        return lax.rem(mf + k, nf)

    def chip_at(j):
        return lax.rem(q + j, nq)

    def chip_from(j):
        return lax.rem(q - j + nq, nq)

    def block(index, size):
        return pl.ds(pl.multiple_of(index * size, size), size)

    def span(c):
        return pl.ds(c * dc, dc)

    direct = n * nf <= DIRECT
    place = me * nf + mf
    ex_peers = [{"ex": ex_at(k)} for k in range(1, n)]
    feat_peers = [{"feat": feat_at(k)} for k in range(1, nf)]
    all_peers = []
    if direct:
        for k in range(1, n * nf):
            index = lax.rem(place + k, n * nf)
            all_peers.append({"ex": index // nf, "feat": lax.rem(index, nf)})

    mass_load = pltpu.make_async_copy(mass_hbm, mass_row, mass_sem)
    mass_load.start()
    own_load = pltpu.make_async_copy(target, tg.at[block(me, t)], own_sem)
    own_load.start()
    loads = []
    for c in range(chunks):
        loads.append(
            pltpu.make_async_copy(train_hbm.at[:, span(c)], train.at[:, span(c)], load_sem.at[c])
        )
        loads[-1].start()

    barrier = pltpu.get_barrier_semaphore()
    greeted = all_peers if direct else ex_peers + feat_peers
    for peer in greeted:
        pl.semaphore_signal(barrier, inc=1, device_id=peer, device_id_type=MESH)
    pl.semaphore_wait(barrier, len(greeted))

    gathers = []
    forwards = []
    for c in range(chunks):
        for j in range(1, nq):
            copy = remote(
                target.at[:, span(c)], tg.at[block(me, t), span(c)],
                g_send.at[c, j], g_recv.at[c, j], "ex", 2 * chip_at(j) + core,
            )
            copy.start()
            gathers.append(copy)
        copy = remote(
            target.at[:, span(c)], tg.at[block(me, t), span(c)],
            f_send.at[c, 0], f_recv.at[c, 0], "ex", sibling,
        )
        copy.start()
        forwards.append([copy])

    mass_load.wait()
    mass_total = jnp.sum(mass_row[...], axis=1, keepdims=True)
    log_b = jnp.log(mass_row[...]) - jnp.log(mass_total)
    mass_col[...] = jnp.broadcast_to(mass_row[...] / mass_total, (8, nt)).T
    own_load.wait()

    def forward(c):
        for j in range(1, nq):
            gathers[c * (nq - 1) + j - 1].wait_recv()
            where = block(2 * chip_from(j) + core, t)
            copy = remote(
                tg.at[where, span(c)], tg.at[where, span(c)],
                f_send.at[c, j], f_recv.at[c, j], "ex", sibling,
            )
            copy.start()
            forwards[c].append(copy)

    def score(c, index):
        where = block(index, rf)
        value = lax.dot_general(
            train[where, c * dc:(c + 1) * dc],
            tg[:, c * dc:(c + 1) * dc],
            (((1,), (1,)), ((), ())),
            preferred_element_type=jnp.float32,
        )
        if c == 0:
            part[where, :] = value
        else:
            part[where, :] += value

    reduces = []
    forward(0)
    for c in range(chunks):
        if c + 1 < chunks:
            forward(c + 1)
        loads[c].wait()
        for copy in forwards[c]:
            copy.wait_recv()
        if c < chunks - 1:
            @pl.loop(0, nf)
            def _(index):
                score(c, index)
        else:
            for k in range(1, nf):
                score(c, feat_at(k))
                copy = remote(
                    part.at[block(feat_at(k), rf)], rs.at[k],
                    r_send.at[k], r_recv.at[k], "feat", feat_at(k),
                )
                copy.start()
                reduces.append(copy)
            score(c, mf)
    logits = part[block(mf, rf), :]
    for copy in reduces:
        copy.wait_recv()
    for k in range(1, nf):
        logits = logits + rs[k]
    logits = logits * scale
    scores[block(mf, rf), :] = logits
    spreads = []
    for k in range(1, nf):
        copy = remote(
            scores.at[block(mf, rf)], scores.at[block(mf, rf)],
            a_send.at[k], a_recv.at[k], "feat", feat_at(k),
        )
        spreads.append(copy)

    def row_lse(value):
        top = jnp.max(value, axis=1, keepdims=True)
        return top + jnp.log(jnp.sum(jnp.exp(value - top), axis=1, keepdims=True))

    def exchange(step, send, recv, here, peers, send_sem, recv_sem, top, total, beside):
        send[step, 0:1, :] = top
        send[step, 1:2, :] = total
        wave = []
        for k, peer in enumerate(peers):
            copy = remote(
                send.at[step], recv.at[step, here],
                send_sem.at[step, k], recv_sem.at[step, k], None, peer,
            )
            copy.start()
            wave.append(copy)
        recv[step, here] = send[step]
        beside()
        for copy in wave:
            copy.wait_recv()
        tops = recv[step, :, 0, :]
        top = jnp.max(tops, axis=0, keepdims=True)
        total = jnp.sum(recv[step, :, 1, :] * jnp.exp(tops - top), axis=0, keepdims=True)
        return top, total, wave

    col_pot = jnp.zeros((1, nt), jnp.float32)
    stats = []
    for step in range(ITERS):
        row_pot = log_a - row_lse(logits + col_pot)
        value = logits + row_pot
        top = jnp.max(value, axis=0, keepdims=True)
        total = jnp.sum(jnp.exp(value - top), axis=0, keepdims=True)

        def beside(step=step, col_pot=col_pot):
            if step == 0:
                for copy in spreads:
                    copy.start()
            if step == ITERS - 1:
                for copy in spreads:
                    copy.wait_recv()

                @pl.loop(0, nf)
                def _(index):
                    full = scores[block(index, rf), :]
                    expo[block(index, rf), :] = full + (log_a - row_lse(full + col_pot))

        if not direct:
            top, total, wave = exchange(
                step, ft_send, ft_recv, mf, feat_peers, t_send, t_recv, top, total, lambda: None
            )
            stats += wave
        top, total, wave = exchange(
            step, ex_send, ex_recv, place if direct else me,
            all_peers if direct else ex_peers, s_send, s_recv, top, total, beside,
        )
        stats += wave
        col_pot = log_b - (top + jnp.log(total))

    for f in range(nf):
        here = slice(f * rf, (f + 1) * rf)
        plan_t[:, here] = jnp.exp(expo[here, :] + col_pot).T.astype(jnp.bfloat16)

    tile = math.gcd(dc, 256)
    swaps = []
    mixes = []

    def mix(c):
        @pl.loop(0, dc // tile)
        def _(index):
            where = pl.ds(pl.multiple_of(c * dc + index * tile, tile), tile)
            value = jnp.dot(plan_t[...], train[:, where], preferred_element_type=jnp.float32)
            value = value.reshape(nq, 2, t, tile)
            macc[:, :, :, where] = value
            mb[:, :, :, where] = value.astype(jnp.bfloat16)

        copy = remote(
            mb.at[:, 1 - core, :, span(c)], xr.at[:, :, span(c)],
            x_send.at[c], x_recv.at[c], "ex", sibling,
        )
        copy.start()
        swaps.append(copy)

    def send_on(c):
        cols = slice(c * dc, (c + 1) * dc)
        swaps[c].wait_recv()
        total = macc[:, core, :, cols] + xr[:, :, cols].astype(jnp.float32)
        cb[:, :, cols] = total.astype(jnp.bfloat16)
        for j in range(1, nq):
            copy = remote(
                cb.at[chip_at(j), :, span(c)], mr.at[q, :, span(c)],
                m_send.at[c, j], m_recv.at[c, j], "ex", 2 * chip_at(j) + core,
            )
            copy.start()
            mixes.append(copy)

    for c in range(chunks):
        mix(c)
        if c > 0:
            send_on(c - 1)
    send_on(chunks - 1)

    weight = mass_col[block(me, t), 0:1]
    for c in range(chunks):
        cols = slice(c * dc, (c + 1) * dc)
        total = macc[q, core, :, cols] + xr[q, :, cols].astype(jnp.float32)
        for j in range(1, nq):
            mixes[c * (nq - 1) + j - 1].wait_recv()
        for j in range(1, nq):
            total = total + mr[chip_at(j), :, cols].astype(jnp.float32)
        out[:, cols] = (total / weight).astype(jnp.bfloat16)
    for group in forwards:
        for copy in group:
            copy.wait_send()
    for copy in gathers + reduces + spreads + stats + swaps + mixes:
        copy.wait_send()


def shards(train_grads, target_grads, target_mass):
    n, nf = lax.axis_size("ex"), lax.axis_size("feat")
    rows, depth = train_grads.shape
    t = target_grads.shape[0]
    nt = t * n
    nq = n // 2
    group = n * nf if n * nf <= DIRECT else n
    chunks = 4 if depth % 512 == 0 else 1
    f32, bf16 = jnp.float32, jnp.bfloat16
    vmem = pl.BlockSpec(memory_space=pltpu.VMEM)
    anywhere = pl.BlockSpec(memory_space=pl.ANY)
    dma = pltpu.SemaphoreType.DMA
    return pl.pallas_call(
        functools.partial(kernel, n, nf, chunks),
        out_shape=jax.ShapeDtypeStruct((t, depth), bf16),
        in_specs=[anywhere, anywhere, anywhere],
        out_specs=vmem,
        scratch_shapes=[
            pltpu.VMEM((rows, depth), bf16),
            pltpu.VMEM((nt, depth), bf16),
            pltpu.VMEM((rows, nt), f32),
            pltpu.VMEM((nf, rows // nf, nt), f32),
            pltpu.VMEM((rows, nt), f32),
            pltpu.VMEM((rows, nt), f32),
            pltpu.VMEM((nt, rows), bf16),
            pltpu.VMEM((nq, 2, t, depth), f32),
            pltpu.VMEM((nq, 2, t, depth), bf16),
            pltpu.VMEM((nq, t, depth), bf16),
            pltpu.VMEM((nq, t, depth), bf16),
            pltpu.VMEM((nq, t, depth), bf16),
            pltpu.VMEM((1, nt), f32),
            pltpu.VMEM((nt, 8), f32),
            pltpu.VMEM((ITERS, 2, nt), f32),
            pltpu.VMEM((ITERS, nf, 2, nt), f32),
            pltpu.VMEM((ITERS, 2, nt), f32),
            pltpu.VMEM((ITERS, group, 2, nt), f32),
            dma((chunks,)), dma, dma,
            dma((chunks, nq)), dma((chunks, nq)),
            dma((chunks, nq)), dma((chunks, nq)),
            dma((nf,)), dma((nf,)),
            dma((ITERS, nf)), dma((ITERS, nf)),
            dma((ITERS, group)), dma((ITERS, group)),
            dma((nf,)), dma((nf,)),
            dma((chunks,)), dma((chunks,)),
            dma((chunks, nq)), dma((chunks, nq)),
        ],
        compiler_params=pltpu.CompilerParams(
            collective_id=0, has_side_effects=True, vmem_limit_bytes=48 * 1024 * 1024
        ),
        cost_estimate=pl.CostEstimate(
            flops=4 * rows * nt * depth,
            bytes_accessed=2 * rows * depth,
            transcendentals=7 * rows * nt,
        ),
    )(train_grads, target_grads, target_mass.reshape(1, nt))


def solution(mesh):
    return jax.shard_map(
        shards,
        mesh=mesh,
        in_specs=(P("ex", "feat"), P("ex", "feat"), P()),
        out_specs=P("ex", "feat"),
        check_vma=False,
    )
```

```python
import functools
import math

import jax
import jax.numpy as jnp
from jax import lax
from jax.experimental import pallas as pl
from jax.experimental.pallas import tpu as pltpu
from jax.sharding import PartitionSpec as P

ITERS = 3
MESH = pl.DeviceIdType.MESH


def remote(src, dst, send, recv, axis, peer):
    return pltpu.make_async_remote_copy(
        src_ref=src,
        dst_ref=dst,
        send_sem=send,
        recv_sem=recv,
        device_id=peer if axis is None else {axis: peer},
        device_id_type=MESH,
    )


def kernel(
    n, nf, chunks,
    train_hbm, target, mass_hbm, out,
    train, tg, part, rs, scores, plan_t, macc, mb, xr, cb, mr, mass_row, mass_col,
    ft_send, ft_recv, ex_send, ex_recv,
    load_sem, own_sem, mass_sem, g_send, g_recv, f_send, f_recv, r_send, r_recv,
    t_send, t_recv, s_send, s_recv, a_send, a_recv, x_send, x_recv, m_send, m_recv,
):
    me = lax.axis_index("ex")
    mf = lax.axis_index("feat")
    rows, depth = train.shape
    nt = tg.shape[0]
    t = target.shape[0]
    dc = depth // chunks
    rf = rows // nf
    nq = n // 2
    q = me // 2
    core = lax.rem(me, 2)
    sibling = me + 1 - 2 * core
    scale = 3.0 / math.sqrt(depth * nf)
    log_a = -math.log(rows * n)

    def ex_at(k):
        return lax.rem(me + k, n)

    def feat_at(k):
        return lax.rem(mf + k, nf)

    def chip_at(j):
        return lax.rem(q + j, nq)

    def chip_from(j):
        return lax.rem(q - j + nq, nq)

    def block(index, size):
        return pl.ds(pl.multiple_of(index * size, size), size)

    def span(c):
        return pl.ds(c * dc, dc)

    ex_peers = [{"ex": ex_at(k)} for k in range(1, n)]
    feat_peers = [{"feat": feat_at(k)} for k in range(1, nf)]

    mass_load = pltpu.make_async_copy(mass_hbm, mass_row, mass_sem)
    mass_load.start()
    own_load = pltpu.make_async_copy(target, tg.at[block(me, t)], own_sem)
    own_load.start()
    loads = []
    for c in range(chunks):
        loads.append(
            pltpu.make_async_copy(train_hbm.at[:, span(c)], train.at[:, span(c)], load_sem.at[c])
        )
        loads[-1].start()

    barrier = pltpu.get_barrier_semaphore()
    greeted = ex_peers + feat_peers
    for peer in greeted:
        pl.semaphore_signal(barrier, inc=1, device_id=peer, device_id_type=MESH)
    pl.semaphore_wait(barrier, len(greeted))

    gathers = []
    forwards = []
    for c in range(chunks):
        for j in range(1, nq):
            copy = remote(
                target.at[:, span(c)], tg.at[block(me, t), span(c)],
                g_send.at[c, j], g_recv.at[c, j], "ex", 2 * chip_at(j) + core,
            )
            copy.start()
            gathers.append(copy)
        copy = remote(
            target.at[:, span(c)], tg.at[block(me, t), span(c)],
            f_send.at[c, 0], f_recv.at[c, 0], "ex", sibling,
        )
        copy.start()
        forwards.append([copy])

    mass_load.wait()
    mass_total = jnp.sum(mass_row[...], axis=1, keepdims=True)
    log_b = jnp.log(mass_row[...]) - jnp.log(mass_total)
    mass_col[...] = jnp.broadcast_to(mass_row[...] / mass_total, (8, nt)).T
    own_load.wait()

    def forward(c):
        for j in range(1, nq):
            gathers[c * (nq - 1) + j - 1].wait_recv()
            where = block(2 * chip_from(j) + core, t)
            copy = remote(
                tg.at[where, span(c)], tg.at[where, span(c)],
                f_send.at[c, j], f_recv.at[c, j], "ex", sibling,
            )
            copy.start()
            forwards[c].append(copy)

    def score(c, index):
        where = block(index, rf)
        value = lax.dot_general(
            train[where, c * dc:(c + 1) * dc],
            tg[:, c * dc:(c + 1) * dc],
            (((1,), (1,)), ((), ())),
            preferred_element_type=jnp.float32,
        )
        if c == 0:
            part[where, :] = value
        else:
            part[where, :] += value

    reduces = []
    forward(0)
    for c in range(chunks):
        if c + 1 < chunks:
            forward(c + 1)
        loads[c].wait()
        for copy in forwards[c]:
            copy.wait_recv()
        if c < chunks - 1:
            @pl.loop(0, nf)
            def _(index):
                score(c, index)
        else:
            for k in range(1, nf):
                score(c, feat_at(k))
                copy = remote(
                    part.at[block(feat_at(k), rf)], rs.at[k],
                    r_send.at[k], r_recv.at[k], "feat", feat_at(k),
                )
                copy.start()
                reduces.append(copy)
            score(c, mf)
    logits = part[block(mf, rf), :]
    for copy in reduces:
        copy.wait_recv()
    for k in range(1, nf):
        logits = logits + rs[k]
    logits = logits * scale
    scores[block(mf, rf), :] = logits
    spreads = []
    for k in range(1, nf):
        copy = remote(
            scores.at[block(mf, rf)], scores.at[block(mf, rf)],
            a_send.at[k], a_recv.at[k], "feat", feat_at(k),
        )
        spreads.append(copy)

    def row_lse(value):
        top = jnp.max(value, axis=1, keepdims=True)
        return top + jnp.log(jnp.sum(jnp.exp(value - top), axis=1, keepdims=True))

    def exchange(step, send, recv, here, peers, send_sem, recv_sem, top, total, beside):
        send[step, 0:1, :] = top
        send[step, 1:2, :] = total
        wave = []
        for k, peer in enumerate(peers):
            copy = remote(
                send.at[step], recv.at[step, here],
                send_sem.at[step, k], recv_sem.at[step, k], None, peer,
            )
            copy.start()
            wave.append(copy)
        recv[step, here] = send[step]
        beside()
        for copy in wave:
            copy.wait_recv()
        tops = recv[step, :, 0, :]
        top = jnp.max(tops, axis=0, keepdims=True)
        total = jnp.sum(recv[step, :, 1, :] * jnp.exp(tops - top), axis=0, keepdims=True)
        return top, total, wave

    def spread():
        for copy in spreads:
            copy.start()

    col_pot = jnp.zeros((1, nt), jnp.float32)
    stats = []
    for step in range(ITERS):
        if step == 1:
            for copy in spreads:
                copy.wait_recv()
        known = logits if step == 0 else scores[...]
        row_pot = log_a - row_lse(known + col_pot)
        value = known + row_pot
        top = jnp.max(value, axis=0, keepdims=True)
        total = jnp.sum(jnp.exp(value - top), axis=0, keepdims=True)
        if step == 0:
            top, total, wave = exchange(
                step, ft_send, ft_recv, mf, feat_peers, t_send, t_recv, top, total, spread
            )
            stats += wave
        top, total, wave = exchange(
            step, ex_send, ex_recv, me, ex_peers, s_send, s_recv, top, total, lambda: None
        )
        stats += wave
        col_pot = log_b - (top + jnp.log(total))

    plan = jnp.exp(scores[...] + row_pot + col_pot)
    plan_t[...] = plan.T.astype(jnp.bfloat16)

    tile = math.gcd(dc, 256)
    swaps = []
    mixes = []

    def mix(c):
        @pl.loop(0, dc // tile)
        def _(index):
            where = pl.ds(pl.multiple_of(c * dc + index * tile, tile), tile)
            value = jnp.dot(plan_t[...], train[:, where], preferred_element_type=jnp.float32)
            value = value.reshape(nq, 2, t, tile)
            macc[:, :, :, where] = value
            mb[:, :, :, where] = value.astype(jnp.bfloat16)

        copy = remote(
            mb.at[:, 1 - core, :, span(c)], xr.at[:, :, span(c)],
            x_send.at[c], x_recv.at[c], "ex", sibling,
        )
        copy.start()
        swaps.append(copy)

    def send_on(c):
        cols = slice(c * dc, (c + 1) * dc)
        swaps[c].wait_recv()
        total = macc[:, core, :, cols] + xr[:, :, cols].astype(jnp.float32)
        cb[:, :, cols] = total.astype(jnp.bfloat16)
        for j in range(1, nq):
            copy = remote(
                cb.at[chip_at(j), :, span(c)], mr.at[q, :, span(c)],
                m_send.at[c, j], m_recv.at[c, j], "ex", 2 * chip_at(j) + core,
            )
            copy.start()
            mixes.append(copy)

    for c in range(chunks):
        mix(c)
        if c > 0:
            send_on(c - 1)
    send_on(chunks - 1)

    weight = mass_col[block(me, t), 0:1]
    for c in range(chunks):
        cols = slice(c * dc, (c + 1) * dc)
        total = macc[q, core, :, cols] + xr[q, :, cols].astype(jnp.float32)
        for j in range(1, nq):
            mixes[c * (nq - 1) + j - 1].wait_recv()
        for j in range(1, nq):
            total = total + mr[chip_at(j), :, cols].astype(jnp.float32)
        out[:, cols] = (total / weight).astype(jnp.bfloat16)
    for group in forwards:
        for copy in group:
            copy.wait_send()
    for copy in gathers + reduces + spreads + stats + swaps + mixes:
        copy.wait_send()


def shards(train_grads, target_grads, target_mass):
    n, nf = lax.axis_size("ex"), lax.axis_size("feat")
    rows, depth = train_grads.shape
    t = target_grads.shape[0]
    nt = t * n
    nq = n // 2
    chunks = 4 if depth % 512 == 0 else 1
    f32, bf16 = jnp.float32, jnp.bfloat16
    vmem = pl.BlockSpec(memory_space=pltpu.VMEM)
    anywhere = pl.BlockSpec(memory_space=pl.ANY)
    dma = pltpu.SemaphoreType.DMA
    return pl.pallas_call(
        functools.partial(kernel, n, nf, chunks),
        out_shape=jax.ShapeDtypeStruct((t, depth), bf16),
        in_specs=[anywhere, anywhere, anywhere],
        out_specs=vmem,
        scratch_shapes=[
            pltpu.VMEM((rows, depth), bf16),
            pltpu.VMEM((nt, depth), bf16),
            pltpu.VMEM((rows, nt), f32),
            pltpu.VMEM((nf, rows // nf, nt), f32),
            pltpu.VMEM((rows, nt), f32),
            pltpu.VMEM((nt, rows), bf16),
            pltpu.VMEM((nq, 2, t, depth), f32),
            pltpu.VMEM((nq, 2, t, depth), bf16),
            pltpu.VMEM((nq, t, depth), bf16),
            pltpu.VMEM((nq, t, depth), bf16),
            pltpu.VMEM((nq, t, depth), bf16),
            pltpu.VMEM((1, nt), f32),
            pltpu.VMEM((nt, 8), f32),
            pltpu.VMEM((ITERS, 2, nt), f32),
            pltpu.VMEM((ITERS, nf, 2, nt), f32),
            pltpu.VMEM((ITERS, 2, nt), f32),
            pltpu.VMEM((ITERS, n, 2, nt), f32),
            dma((chunks,)), dma, dma,
            dma((chunks, nq)), dma((chunks, nq)),
            dma((chunks, nq)), dma((chunks, nq)),
            dma((nf,)), dma((nf,)),
            dma((ITERS, nf)), dma((ITERS, nf)),
            dma((ITERS, n)), dma((ITERS, n)),
            dma((nf,)), dma((nf,)),
            dma((chunks,)), dma((chunks,)),
            dma((chunks, nq)), dma((chunks, nq)),
        ],
        compiler_params=pltpu.CompilerParams(
            collective_id=0, has_side_effects=True, vmem_limit_bytes=48 * 1024 * 1024
        ),
        cost_estimate=pl.CostEstimate(
            flops=4 * rows * nt * depth,
            bytes_accessed=2 * rows * depth,
            transcendentals=7 * rows * nt,
        ),
    )(train_grads, target_grads, target_mass.reshape(1, nt))


def solution(mesh):
    return jax.shard_map(
        shards,
        mesh=mesh,
        in_specs=(P("ex", "feat"), P("ex", "feat"), P()),
        out_specs=P("ex", "feat"),
        check_vma=False,
    )
```

```python
import functools
import math

import jax
import jax.numpy as jnp
from jax import lax
from jax.experimental import pallas as pl
from jax.experimental.pallas import tpu as pltpu
from jax.sharding import PartitionSpec as P

ITERS = 3
MESH = pl.DeviceIdType.MESH


def remote(src, dst, send, recv, axis, peer):
    return pltpu.make_async_remote_copy(
        src_ref=src,
        dst_ref=dst,
        send_sem=send,
        recv_sem=recv,
        device_id=peer if axis is None else {axis: peer},
        device_id_type=MESH,
    )


def kernel(
    n, nf, chunks,
    train_hbm, target, mass_hbm, out,
    train, tg, part, rs, scores, plan_t, macc, mb, xr, cb, mr, mass_row, mass_col,
    ft_send, ft_recv, ex_send, ex_recv,
    load_sem, own_sem, mass_sem, g_send, g_recv, f_send, f_recv, r_send, r_recv,
    t_send, t_recv, s_send, s_recv, a_send, a_recv, x_send, x_recv, m_send, m_recv,
):
    me = lax.axis_index("ex")
    mf = lax.axis_index("feat")
    rows, depth = train.shape
    nt = tg.shape[0]
    t = target.shape[0]
    dc = depth // chunks
    rf = rows // nf
    nq = n // 2
    q = me // 2
    core = lax.rem(me, 2)
    sibling = me + 1 - 2 * core
    scale = 3.0 / math.sqrt(depth * nf)
    log_a = -math.log(rows * n)

    def ex_at(k):
        return lax.rem(me + k, n)

    def feat_at(k):
        return lax.rem(mf + k, nf)

    def chip_at(j):
        return lax.rem(q + j, nq)

    def chip_from(j):
        return lax.rem(q - j + nq, nq)

    def block(index, size):
        return pl.ds(pl.multiple_of(index * size, size), size)

    def span(c):
        return pl.ds(c * dc, dc)

    ex_peers = [{"ex": ex_at(k)} for k in range(1, n)]
    feat_peers = [{"feat": feat_at(k)} for k in range(1, nf)]

    mass_load = pltpu.make_async_copy(mass_hbm, mass_row, mass_sem)
    mass_load.start()
    own_load = pltpu.make_async_copy(target, tg.at[block(me, t)], own_sem)
    own_load.start()
    loads = []
    for c in range(chunks):
        loads.append(
            pltpu.make_async_copy(train_hbm.at[:, span(c)], train.at[:, span(c)], load_sem.at[c])
        )
        loads[-1].start()

    barrier = pltpu.get_barrier_semaphore()
    greeted = ex_peers + feat_peers
    for peer in greeted:
        pl.semaphore_signal(barrier, inc=1, device_id=peer, device_id_type=MESH)
    pl.semaphore_wait(barrier, len(greeted))

    gathers = []
    forwards = []
    for c in range(chunks):
        for j in range(1, nq):
            copy = remote(
                target.at[:, span(c)], tg.at[block(me, t), span(c)],
                g_send.at[c, j], g_recv.at[c, j], "ex", 2 * chip_at(j) + core,
            )
            copy.start()
            gathers.append(copy)
        copy = remote(
            target.at[:, span(c)], tg.at[block(me, t), span(c)],
            f_send.at[c, 0], f_recv.at[c, 0], "ex", sibling,
        )
        copy.start()
        forwards.append([copy])

    mass_load.wait()
    mass_total = jnp.sum(mass_row[...], axis=1, keepdims=True)
    log_b = jnp.log(mass_row[...]) - jnp.log(mass_total)
    mass_col[...] = jnp.broadcast_to(mass_row[...] / mass_total, (8, nt)).T
    own_load.wait()

    def forward(c):
        for j in range(1, nq):
            gathers[c * (nq - 1) + j - 1].wait_recv()
            where = block(2 * chip_from(j) + core, t)
            copy = remote(
                tg.at[where, span(c)], tg.at[where, span(c)],
                f_send.at[c, j], f_recv.at[c, j], "ex", sibling,
            )
            copy.start()
            forwards[c].append(copy)

    def score(c, index):
        where = block(index, rf)
        value = lax.dot_general(
            train[where, c * dc:(c + 1) * dc],
            tg[:, c * dc:(c + 1) * dc],
            (((1,), (1,)), ((), ())),
            preferred_element_type=jnp.float32,
        )
        if c == 0:
            part[where, :] = value
        else:
            part[where, :] += value

    reduces = []
    forward(0)
    for c in range(chunks):
        if c + 1 < chunks:
            forward(c + 1)
        loads[c].wait()
        for copy in forwards[c]:
            copy.wait_recv()
        if c < chunks - 1:
            @pl.loop(0, nf)
            def _(index):
                score(c, index)
        else:
            for k in range(1, nf):
                score(c, feat_at(k))
                copy = remote(
                    part.at[block(feat_at(k), rf)], rs.at[k],
                    r_send.at[k], r_recv.at[k], "feat", feat_at(k),
                )
                copy.start()
                reduces.append(copy)
            score(c, mf)
    logits = part[block(mf, rf), :]
    for copy in reduces:
        copy.wait_recv()
    for k in range(1, nf):
        logits = logits + rs[k]
    logits = logits * scale
    scores[block(mf, rf), :] = logits
    spreads = []
    for k in range(1, nf):
        copy = remote(
            scores.at[block(mf, rf)], scores.at[block(mf, rf)],
            a_send.at[k], a_recv.at[k], "feat", feat_at(k),
        )
        copy.start()
        spreads.append(copy)

    def row_lse(value):
        top = jnp.max(value, axis=1, keepdims=True)
        return top + jnp.log(jnp.sum(jnp.exp(value - top), axis=1, keepdims=True))

    def exchange(step, send, recv, here, peers, send_sem, recv_sem, top, total):
        send[step, 0:1, :] = top
        send[step, 1:2, :] = total
        wave = []
        for k, peer in enumerate(peers):
            copy = remote(
                send.at[step], recv.at[step, here],
                send_sem.at[step, k], recv_sem.at[step, k], None, peer,
            )
            copy.start()
            wave.append(copy)
        recv[step, here] = send[step]
        for copy in wave:
            copy.wait_recv()
        tops = recv[step, :, 0, :]
        top = jnp.max(tops, axis=0, keepdims=True)
        total = jnp.sum(recv[step, :, 1, :] * jnp.exp(tops - top), axis=0, keepdims=True)
        return top, total, wave

    col_pot = jnp.zeros((1, nt), jnp.float32)
    stats = []
    for step in range(ITERS):
        if step == 1:
            for copy in spreads:
                copy.wait_recv()
        known = logits if step == 0 else scores[...]
        row_pot = log_a - row_lse(known + col_pot)
        value = known + row_pot
        top = jnp.max(value, axis=0, keepdims=True)
        total = jnp.sum(jnp.exp(value - top), axis=0, keepdims=True)
        if step == 0:
            top, total, wave = exchange(
                step, ft_send, ft_recv, mf, feat_peers, t_send, t_recv, top, total
            )
            stats += wave
        top, total, wave = exchange(
            step, ex_send, ex_recv, me, ex_peers, s_send, s_recv, top, total
        )
        stats += wave
        col_pot = log_b - (top + jnp.log(total))

    plan = jnp.exp(scores[...] + row_pot + col_pot)
    plan_t[...] = plan.T.astype(jnp.bfloat16)

    tile = math.gcd(dc, 256)
    swaps = []
    mixes = []

    def mix(c):
        @pl.loop(0, dc // tile)
        def _(index):
            where = pl.ds(pl.multiple_of(c * dc + index * tile, tile), tile)
            value = jnp.dot(plan_t[...], train[:, where], preferred_element_type=jnp.float32)
            value = value.reshape(nq, 2, t, tile)
            macc[:, :, :, where] = value
            mb[:, :, :, where] = value.astype(jnp.bfloat16)

        copy = remote(
            mb.at[:, 1 - core, :, span(c)], xr.at[:, :, span(c)],
            x_send.at[c], x_recv.at[c], "ex", sibling,
        )
        copy.start()
        swaps.append(copy)

    def send_on(c):
        cols = slice(c * dc, (c + 1) * dc)
        swaps[c].wait_recv()
        total = macc[:, core, :, cols] + xr[:, :, cols].astype(jnp.float32)
        cb[:, :, cols] = total.astype(jnp.bfloat16)
        for j in range(1, nq):
            copy = remote(
                cb.at[chip_at(j), :, span(c)], mr.at[q, :, span(c)],
                m_send.at[c, j], m_recv.at[c, j], "ex", 2 * chip_at(j) + core,
            )
            copy.start()
            mixes.append(copy)

    for c in range(chunks):
        mix(c)
        if c > 0:
            send_on(c - 1)
    send_on(chunks - 1)

    weight = mass_col[block(me, t), 0:1]
    for c in range(chunks):
        cols = slice(c * dc, (c + 1) * dc)
        total = macc[q, core, :, cols] + xr[q, :, cols].astype(jnp.float32)
        for j in range(1, nq):
            mixes[c * (nq - 1) + j - 1].wait_recv()
        for j in range(1, nq):
            total = total + mr[chip_at(j), :, cols].astype(jnp.float32)
        out[:, cols] = (total / weight).astype(jnp.bfloat16)
    for group in forwards:
        for copy in group:
            copy.wait_send()
    for copy in gathers + reduces + spreads + stats + swaps + mixes:
        copy.wait_send()


def shards(train_grads, target_grads, target_mass):
    n, nf = lax.axis_size("ex"), lax.axis_size("feat")
    rows, depth = train_grads.shape
    t = target_grads.shape[0]
    nt = t * n
    nq = n // 2
    chunks = 4 if depth % 512 == 0 else 1
    f32, bf16 = jnp.float32, jnp.bfloat16
    vmem = pl.BlockSpec(memory_space=pltpu.VMEM)
    anywhere = pl.BlockSpec(memory_space=pl.ANY)
    dma = pltpu.SemaphoreType.DMA
    return pl.pallas_call(
        functools.partial(kernel, n, nf, chunks),
        out_shape=jax.ShapeDtypeStruct((t, depth), bf16),
        in_specs=[anywhere, anywhere, anywhere],
        out_specs=vmem,
        scratch_shapes=[
            pltpu.VMEM((rows, depth), bf16),
            pltpu.VMEM((nt, depth), bf16),
            pltpu.VMEM((rows, nt), f32),
            pltpu.VMEM((nf, rows // nf, nt), f32),
            pltpu.VMEM((rows, nt), f32),
            pltpu.VMEM((nt, rows), bf16),
            pltpu.VMEM((nq, 2, t, depth), f32),
            pltpu.VMEM((nq, 2, t, depth), bf16),
            pltpu.VMEM((nq, t, depth), bf16),
            pltpu.VMEM((nq, t, depth), bf16),
            pltpu.VMEM((nq, t, depth), bf16),
            pltpu.VMEM((1, nt), f32),
            pltpu.VMEM((nt, 8), f32),
            pltpu.VMEM((ITERS, 2, nt), f32),
            pltpu.VMEM((ITERS, nf, 2, nt), f32),
            pltpu.VMEM((ITERS, 2, nt), f32),
            pltpu.VMEM((ITERS, n, 2, nt), f32),
            dma((chunks,)), dma, dma,
            dma((chunks, nq)), dma((chunks, nq)),
            dma((chunks, nq)), dma((chunks, nq)),
            dma((nf,)), dma((nf,)),
            dma((ITERS, nf)), dma((ITERS, nf)),
            dma((ITERS, n)), dma((ITERS, n)),
            dma((nf,)), dma((nf,)),
            dma((chunks,)), dma((chunks,)),
            dma((chunks, nq)), dma((chunks, nq)),
        ],
        compiler_params=pltpu.CompilerParams(
            collective_id=0, has_side_effects=True, vmem_limit_bytes=48 * 1024 * 1024
        ),
        cost_estimate=pl.CostEstimate(
            flops=4 * rows * nt * depth,
            bytes_accessed=2 * rows * depth,
            transcendentals=7 * rows * nt,
        ),
    )(train_grads, target_grads, target_mass.reshape(1, nt))


def solution(mesh):
    return jax.shard_map(
        shards,
        mesh=mesh,
        in_specs=(P("ex", "feat"), P("ex", "feat"), P()),
        out_specs=P("ex", "feat"),
        check_vma=False,
    )
```
